512 devices in a mesh: rows: 128 (over z_hi, y, x), grp: 4 (over z_lo, core).
Axes of the slice: x: 4, y: 8, z: 8 (z_hi: 4, z_lo: 2; z = z_hi * 2 + z_lo), core: 2. Of those that a mesh axis runs over, the one named last changes fastest.
Arguments:
- features: bfloat16 [131072, 2048], P('rows', 'grp'), may hold values from -48 to 48
- clusters: int32 [131072], replicated, may hold values from 0 to 63, as said below
- bands: int32 [512], P('rows'), may hold values from 1 to 12, as said below
Outputs:
- max_cos: float32 [131072], P(('rows', 'grp'))
- dup_score: float32 [131072], P(('rows', 'grp'))
The draws below stay inside these ranges and needn't reach their ends.
Inputs may be any that keep to these rules, and one draw needn't show every extreme that they name: `clusters`: ids never fall along the rows, start at 0 and rise by one where a new cluster begins. `bands`: some block has the width 12 in every draw.
All inputs are finite; a program needn't handle non-finite values.
Results may differ from the reference program's by a relative error of at most 0.0003.
Values may be sent and summed in bfloat16 or wider, within the bound.
A program may use at most 64 MiB of HBM per device.

```python
import math
import jax
import jax.numpy as jnp
from jax import lax

F = 2048
BLOCK = 256
BAND = 12
ROWS = 131072
NBLK = 512


def draw_features(key, part):
    key = jax.random.fold_in(key, 13)
    keys_all = jax.random.split(key, 7)
    base = jax.random.normal(keys_all[0], (ROWS, F), jnp.float32)
    noise = jax.random.normal(keys_all[3], (ROWS, F), jnp.float32)
    lowest = math.log(0.01)
    copies = jax.random.randint(keys_all[4], (ROWS,), 0, 4) == 0
    spacing = jax.random.randint(keys_all[5], (ROWS,), 1, (BAND + 1) * BLOCK)
    source = jnp.maximum(jnp.arange(ROWS, dtype=jnp.int32) - spacing, 0)
    strength = jnp.exp(jax.random.uniform(keys_all[6], (ROWS, 1), jnp.float32, lowest, math.log(0.3)))
    twins = base[source] + strength * noise
    result = jnp.where(copies[:, None], twins, base)
    return jnp.clip(result, -48.0, 48.0).astype(jnp.bfloat16)


def draw_clusters(key, part):
    key = jax.random.fold_in(key, 11)
    starts_count = max(1, ROWS // (8 * BLOCK)) - 1
    order = jax.random.permutation(key, ROWS - 1).astype(jnp.int32)
    chosen = order[:starts_count] + 1
    fresh = jnp.zeros((ROWS,), jnp.int32).at[chosen].set(1)
    return jnp.cumsum(fresh).astype(jnp.int32)


def draw_bands(key, part):
    key = jax.random.fold_in(key, 12)
    key_one, key_two, key_spot = jax.random.split(key, 3)
    earlier = jax.random.randint(key_one, (NBLK,), 1, BAND + 1)
    another = jax.random.randint(key_two, (NBLK,), 1, BAND + 1)
    widths = jnp.minimum(earlier, another)
    spot = jax.random.randint(key_spot, (), 0, NBLK)
    return widths.at[spot].set(BAND).astype(jnp.int32)


def setup_inputs(seed: int = 0) -> dict:
    key_list = jax.random.split(jax.random.key(seed), 4)
    features = draw_features(jax.random.fold_in(key_list[3], 71), 0)
    clusters = draw_clusters(jax.random.fold_in(key_list[3], 71), 0)
    bands = draw_bands(jax.random.fold_in(key_list[3], 71), 0)
    return {"features": features, "clusters": clusters, "bands": bands}


SHARPNESS = 256.0
EPSILON = 1e-06

def merge_stats(former, latter):
    cos_former, sum_former = former
    cos_latter, sum_latter = latter
    cos_both = jnp.maximum(cos_former, cos_latter)
    base_both = jnp.maximum(0.0, SHARPNESS * cos_both)
    sum_both = sum_former * jnp.exp(jnp.maximum(0.0, SHARPNESS * cos_former) - base_both) + sum_latter * jnp.exp(jnp.maximum(0.0, SHARPNESS * cos_latter) - base_both)
    return (cos_both, sum_both)

def masked_stats(cosine, chosen, axis):
    top_cos = lax.optimization_barrier(jnp.max(jnp.where(chosen, cosine, -1.0), axis=axis))
    base_exp = jnp.maximum(0.0, SHARPNESS * top_cos)
    exponent = jnp.where(chosen, SHARPNESS * cosine - jnp.expand_dims(base_exp, axis), -10000.0)
    return (top_cos, lax.optimization_barrier(jnp.sum(jnp.exp(exponent), axis=axis)))

def finish(top_cos, summed):
    base_exp = jnp.maximum(0.0, SHARPNESS * top_cos)
    return base_exp + jnp.log(jnp.exp(-base_exp) + summed)

def reference(features, clusters, bands):
    window = (BAND + 1) * BLOCK
    padding = BAND * BLOCK
    padded = jnp.pad(features, ((0, padding), (0, 0)))
    inverse = lax.rsqrt(lax.optimization_barrier(jnp.sum(jnp.square(padded.astype(jnp.float32)), axis=1)) + EPSILON)
    labels = jnp.pad(clusters, (0, padding), constant_values=-1)
    positions = jnp.arange(window, dtype=jnp.int32)
    in_block = jnp.arange(BLOCK, dtype=jnp.int32)

    def advance(running, block_id):
        top_all, sum_all = running
        first_row = (block_id * BLOCK).astype(jnp.int32)
        query_feats = lax.dynamic_slice_in_dim(padded, first_row, BLOCK, 0)
        key_feats = lax.dynamic_slice_in_dim(padded, first_row, window, 0)
        products = jnp.dot(query_feats, key_feats.T, preferred_element_type=jnp.float32)
        cosine = products * lax.dynamic_slice_in_dim(inverse, first_row, BLOCK)[:, None] * lax.dynamic_slice_in_dim(inverse, first_row, window)[None, :]
        same_group = lax.dynamic_slice_in_dim(labels, first_row, BLOCK)[:, None] == lax.dynamic_slice_in_dim(labels, first_row, window)[None, :]
        key_block = block_id + positions // BLOCK
        forward = (key_block > block_id) & (key_block <= block_id + bands[block_id])
        same_block = (key_block[None, :] == block_id) & (positions[None, :] != in_block[:, None])
        row_top, row_sum = masked_stats(cosine, same_group & (forward[None, :] | same_block), 1)
        col_top, col_sum = masked_stats(cosine, same_group & forward[None, :], 0)
        window_stats = merge_stats((lax.dynamic_slice_in_dim(top_all, first_row, window), lax.dynamic_slice_in_dim(sum_all, first_row, window)), (col_top, col_sum))
        head_stats = merge_stats((window_stats[0][:BLOCK], window_stats[1][:BLOCK]), (row_top, row_sum))
        new_top = jnp.concatenate([head_stats[0], window_stats[0][BLOCK:]])
        new_sum = jnp.concatenate([head_stats[1], window_stats[1][BLOCK:]])
        top_all = lax.dynamic_update_slice_in_dim(top_all, new_top, first_row, 0)
        sum_all = lax.dynamic_update_slice_in_dim(sum_all, new_sum, first_row, 0)
        return ((top_all, sum_all), None)
    start_state = (jnp.full((ROWS + padding,), -1.0, jnp.float32), jnp.zeros((ROWS + padding,), jnp.float32))
    (top_all, sum_all), unused_out = lax.scan(advance, start_state, jnp.arange(NBLK, dtype=jnp.int32))
    max_cos = top_all[:ROWS]
    return (max_cos, finish(max_cos, sum_all[:ROWS]))
```

```python
import functools
import math

import jax
import jax.numpy as jnp
from jax import lax
from jax.experimental import pallas as pl
from jax.experimental.pallas import tpu as pltpu
from jax.sharding import PartitionSpec as P

MESH = pl.DeviceIdType.MESH
BLOCK = 256
SHARPNESS = 256.0
EPSILON = 1e-06
SCALE = SHARPNESS * math.log2(math.e)
MASKED = -1e30

NEXT1, NEXT2, NEXT3, PASS1, PASS2 = range(5)
ORDER = (0, 1, 3, 2)


def as_row(column):
    return jnp.transpose(jnp.broadcast_to(column, (column.shape[0], 128)))[0:1, :]


def as_column(row):
    return jnp.transpose(jnp.broadcast_to(row, (128, row.shape[1])))[:, 0:1]


def merge(former, latter):
    top = jnp.maximum(former[0], latter[0])
    base = jnp.maximum(0.0, top)
    summed = former[1] * jnp.exp2(jnp.maximum(0.0, former[0]) - base) + latter[1] * jnp.exp2(
        jnp.maximum(0.0, latter[0]) - base
    )
    return (top, summed)


def kernel(
    runs,
    features,
    clusters,
    bands,
    top_out,
    score_out,
    whole,
    ahead,
    work,
    labels,
    key_msg,
    key_got,
    query_msg,
    query_got,
    load_sem,
    label_sem,
    whole_send,
    whole_recv,
    pass_send,
    ahead_send,
    ahead_recv,
    key_send,
    key_recv,
    query_send,
    query_recv,
):
    p = lax.axis_index("rows")
    m = lax.axis_index("grp")
    core = m % 2
    column = p % 4
    ring = p - column

    def at(run, member):
        return {"rows": run, "grp": member}

    def mate(j):
        low = (m + j) % 2
        high = (m // 2 + j // 2) % 2
        return high * 2 + low

    def shifted(distance):
        return (p + distance + runs) % runs

    left = ring + (column + 3) % 4
    right = ring + (column + 1) % 4
    below = shifted(-4)
    above = shifted(4)

    loads = []
    for j in range(4):
        start = pl.multiple_of(mate(j) * BLOCK, BLOCK)
        loads.append(
            pltpu.make_async_copy(features.at[pl.ds(start, BLOCK)], whole.at[0, j], load_sem.at[j])
        )
    for j in (1, 3, 2, 0):
        loads[j].start()
    label_loads = []
    for i in range(4):
        start = pl.multiple_of(shifted(i) * 8, 8)
        label_loads.append(
            pltpu.make_async_copy(clusters.at[pl.ds(start, 8)], labels.at[i], label_sem.at[i])
        )
        label_loads[i].start()

    barrier = pltpu.get_barrier_semaphore()
    greeted = [at(p, mate(j)) for j in (1, 2, 3)]
    greeted += [at(run, m) for run in (left, right, above, shifted(-1), shifted(-2), shifted(-3))]
    for device in greeted:
        pl.semaphore_signal(barrier, inc=1, device_id=device, device_id_type=MESH)
    for j in range(4):
        loads[j].wait()
    pl.semaphore_wait(barrier, len(greeted))

    def group_copy(piece, j, to_piece, to_j, partner, send_sem):
        return pltpu.make_async_remote_copy(
            src_ref=whole.at[piece, j],
            dst_ref=whole.at[to_piece, to_j],
            send_sem=send_sem,
            recv_sem=whole_recv.at[to_piece, to_j],
            device_id=at(p, mate(partner)),
            device_id_type=MESH,
        )

    def to_core(j):
        return group_copy(0, j, 1, j ^ 1, 1, whole_send.at[0, j])

    def to_chip(j):
        return group_copy(0, j, 2, j ^ 2, 2, whole_send.at[1, j])

    def pass_on(j):
        return group_copy(2, j, 3, j ^ 1, 1, pass_send.at[j])

    def arrived(piece, j):
        group_copy(0, j, piece, j, 1, whole_send.at[0, 0]).wait_recv()

    def ahead_copy(kind, source, r, run, slot):
        return pltpu.make_async_remote_copy(
            src_ref=source,
            dst_ref=ahead.at[slot, r],
            send_sem=ahead_send.at[kind, r],
            recv_sem=ahead_recv.at[slot, r],
            device_id=at(run, m),
            device_id_type=MESH,
        )

    def ahead_arrived(slot, r):
        ahead_copy(0, whole.at[0, 0], r, p, slot).wait_recv()

    even, odd = core == 0, core == 1

    def send_own(r):
        own = whole.at[r, 0]

        @pl.when(column != 0)
        def _():
            ahead_copy(0, own, r, left, NEXT1).start()

        @pl.when((even & (column == 3)) | (odd & (column >= 2)))
        def _():
            slot = jnp.where(odd & (column == 2), PASS1, NEXT3)
            ahead_copy(2, own, r, right, slot).start()

        @pl.when((even & (column < 3)) | (odd & (column < 2)))
        def _():
            ahead_copy(3, own, r, below, PASS1).start()

    def relay_pass(r):
        passing = ahead.at[PASS1, r]

        @pl.when((even & (column < 3)) | (odd & (column != 2)))
        def _():
            ahead_arrived(PASS1, r)

        @pl.when(column == 0)
        def _():
            ahead_copy(0, passing, r, left, NEXT1).start()

        @pl.when((even & (column < 3)) | (odd & (column < 2)))
        def _():
            ahead_copy(2, passing, r, right, NEXT3).start()

        @pl.when(odd & (column == 3))
        def _():
            ahead_copy(3, passing, r, below, NEXT3).start()
            ahead_copy(1, passing, r, right, NEXT2).start()

    def relay_next(r):
        @pl.when(even)
        def _():
            ahead_arrived(NEXT1, r)

            @pl.when(column == 0)
            def _():
                ahead_copy(4, ahead.at[NEXT1, r], r, below, PASS2).start()

            @pl.when(column != 0)
            def _():
                ahead_copy(1, ahead.at[NEXT1, r], r, left, NEXT2).start()

        @pl.when(odd & (column < 3))
        def _():
            ahead_arrived(NEXT3, r)
            ahead_copy(1, ahead.at[NEXT3, r], r, right, NEXT2).start()

    def relay_second(r):
        @pl.when(even & (column == 0))
        def _():
            ahead_arrived(PASS2, r)
            ahead_copy(1, ahead.at[PASS2, r], r, left, NEXT2).start()

    to_core(1).start()
    to_chip(3).start()
    to_chip(2).start()
    send_own(0)
    for j in (0, 2, 3):
        to_core(j).start()
    arrived(1, 0)
    send_own(1)
    relay_pass(0)
    arrived(2, 1)
    pass_on(1).start()
    arrived(3, 0)
    send_own(3)
    relay_pass(1)
    arrived(2, 0)
    send_own(2)
    pass_on(0).start()
    to_chip(3).wait_send()
    to_chip(2).wait_send()
    to_chip(1).start()
    to_chip(0).start()
    relay_pass(3)
    relay_next(0)
    relay_pass(2)
    relay_next(1)
    arrived(2, 2)
    pass_on(2).start()
    relay_next(3)
    arrived(2, 3)
    pass_on(3).start()
    relay_next(2)
    for r in ORDER:
        relay_second(r)

    for j in (1, 2, 3):
        arrived(1, j)
    for j in (1, 2, 3):
        arrived(3, j)
    for i in range(4):
        label_loads[i].wait()

    def inverse_norm(blocks):
        squares = [jnp.square(b.astype(jnp.float32)) for b in blocks]
        return lax.rsqrt(
            jnp.sum(squares[0] + squares[1] + squares[2] + squares[3], axis=1, keepdims=True)
            + EPSILON
        )

    def label_row(i, block):
        return jnp.concatenate(
            [labels[i, pl.ds(2 * block, 1), :], labels[i, pl.ds(2 * block + 1, 1), :]], axis=1
        )

    query_inv, query_label = [], []
    own_inv = None
    for j in range(4):
        inv = inverse_norm([whole[r, j] for r in range(4)])
        own_inv = inv if j == 0 else own_inv
        query_inv.append(as_row(inv))
        query_label.append(label_row(0, mate(j)))

    def tile(i, keys, inv):
        label = as_column(label_row(i, m).astype(jnp.float32)).astype(jnp.int32)
        label = jnp.where(p + i < runs, label, -2)
        key_scale = inv * SCALE
        key_top = jnp.full((BLOCK, 1), MASKED, jnp.float32)
        key_sum = jnp.zeros((BLOCK, 1), jnp.float32)
        tops = []
        for j in range(4):
            products = None
            for r in range(4):
                term = lax.dot_general(
                    keys[r], whole[r, j], (((1,), (1,)), ((), ())), preferred_element_type=jnp.float32
                )
                products = term if products is None else products + term
            block = mate(j)
            if i > 0:
                valid = 4 * i + m - block <= bands[block]
            elif j > 0:
                valid = jnp.where(block > m, block - m <= bands[m], m - block <= bands[block])
            else:
                valid = True
            query = query_label[j] if valid is True else jnp.where(valid, query_label[j], -1)
            chosen = label == query
            if i == 0 and j == 0:
                rows = lax.broadcasted_iota(jnp.int32, (BLOCK, BLOCK), 0)
                columns = lax.broadcasted_iota(jnp.int32, (BLOCK, BLOCK), 1)
                chosen = chosen & (rows != columns)
            scaled = jnp.where(chosen, products * key_scale * query_inv[j], MASKED)
            work[:, j * BLOCK : (j + 1) * BLOCK] = scaled
            key_top = jnp.maximum(key_top, jnp.max(scaled, axis=1, keepdims=True))
            if i > 0:
                tops.append(jnp.max(scaled, axis=0, keepdims=True))
        key_base = jnp.maximum(0.0, key_top)
        sums = []
        for j in range(4):
            scaled = work[:, j * BLOCK : (j + 1) * BLOCK]
            key_sum += jnp.sum(jnp.exp2(scaled - key_base), axis=1, keepdims=True)
            if i > 0:
                base = jnp.maximum(0.0, tops[j])
                sums.append(jnp.sum(jnp.exp2(scaled - base), axis=0, keepdims=True))
        return (as_row(key_top), as_row(key_sum)), list(zip(tops, sums))

    own, _ = tile(0, [whole[r, 0] for r in range(4)], own_inv)

    def key_copy(i):
        return pltpu.make_async_remote_copy(
            src_ref=key_msg.at[i - 1],
            dst_ref=key_got.at[i - 1],
            send_sem=key_send.at[i - 1],
            recv_sem=key_recv.at[i - 1],
            device_id=at(shifted(i), m),
            device_id_type=MESH,
        )

    def query_copy(j):
        return pltpu.make_async_remote_copy(
            src_ref=query_msg.at[j - 1],
            dst_ref=query_got.at[j - 1],
            send_sem=query_send.at[j - 1],
            recv_sem=query_recv.at[j - 1],
            device_id=at(p, mate(j)),
            device_id_type=MESH,
        )

    running = None
    for i, slot in ((1, NEXT1), (3, NEXT3), (2, NEXT2)):
        for r in ORDER:
            if slot == NEXT1:
                @pl.when(odd)
                def _():
                    ahead_arrived(NEXT1, r)
            elif slot == NEXT3:
                @pl.when(even | (column == 3))
                def _():
                    ahead_arrived(NEXT3, r)
            else:
                ahead_arrived(NEXT2, r)
        keys = [ahead[slot, r] for r in range(4)]
        key_stats, query_stats = tile(i, keys, inverse_norm(keys))
        key_msg[i - 1, 0:1, :] = key_stats[0]
        key_msg[i - 1, 1:2, :] = key_stats[1]
        key_copy(i).start()
        if running is None:
            running = query_stats
        else:
            running = [merge(a, b) for a, b in zip(running, query_stats)]

    for j in (3, 2, 1):
        query_msg[j - 1, 0:1, :] = running[j][0]
        query_msg[j - 1, 1:2, :] = running[j][1]
        query_copy(j).start()
    state = merge(own, running[0])

    for r in range(4):
        ahead_copy(0, whole.at[0, 0], r, p, NEXT1).wait_send()
        ahead_copy(1, whole.at[0, 0], r, p, NEXT1).wait_send()
        ahead_copy(2, whole.at[0, 0], r, p, NEXT1).wait_send()

        @pl.when((even & (column < 3)) | (odd & (column != 2)))
        def _():
            ahead_copy(3, whole.at[0, 0], r, p, NEXT1).wait_send()

        @pl.when(even & (column == 0))
        def _():
            ahead_copy(4, whole.at[0, 0], r, p, NEXT1).wait_send()

    for j in range(4):
        to_core(j).wait_send()
        pass_on(j).wait_send()
    to_chip(1).wait_send()
    to_chip(0).wait_send()
    for i in (1, 3, 2):
        key_copy(i).wait()
        state = merge(state, (key_got[i - 1, 0:1, :], key_got[i - 1, 1:2, :]))
    for j in (1, 2, 3):
        query_copy(j).wait()
        state = merge(state, (query_got[j - 1, 0:1, :], query_got[j - 1, 1:2, :]))
    top, summed = state
    base = jnp.maximum(0.0, top)
    top_out[...] = jnp.maximum(-1.0, top * (1.0 / SCALE))
    score_out[...] = base * math.log(2.0) + jnp.log(jnp.exp2(-base) + summed)


def on_device(features, clusters, bands):
    runs = lax.axis_size("rows")
    rows, width = features.shape
    dma = pltpu.SemaphoreType.DMA
    top, score = pl.pallas_call(
        functools.partial(kernel, runs),
        out_shape=[jax.ShapeDtypeStruct((1, BLOCK), jnp.float32)] * 2,
        in_specs=[
            pl.BlockSpec(memory_space=pl.ANY),
            pl.BlockSpec(memory_space=pl.ANY),
            pl.BlockSpec(memory_space=pltpu.SMEM),
        ],
        out_specs=[pl.BlockSpec(memory_space=pltpu.VMEM)] * 2,
        scratch_shapes=[
            pltpu.VMEM((4, 4, BLOCK, width), jnp.bfloat16),
            pltpu.VMEM((5, 4, BLOCK, width), jnp.bfloat16),
            pltpu.VMEM((BLOCK, rows), jnp.float32),
            pltpu.VMEM((4, 8, 128), jnp.int32),
            pltpu.VMEM((3, 8, BLOCK), jnp.float32),
            pltpu.VMEM((3, 8, BLOCK), jnp.float32),
            pltpu.VMEM((3, 8, BLOCK), jnp.float32),
            pltpu.VMEM((3, 8, BLOCK), jnp.float32),
            dma((4,)),
            dma((4,)),
            dma((2, 4)),
            dma((4, 4)),
            dma((4,)),
            dma((5, 4)),
            dma((5, 4)),
            dma((3,)),
            dma((3,)),
            dma((3,)),
            dma((3,)),
        ],
        compiler_params=pltpu.CompilerParams(
            collective_id=0, has_side_effects=True, vmem_limit_bytes=48 * 1024 * 1024
        ),
        name="screen",
    )(features, clusters.reshape(-1, 128), bands)
    return (top.reshape(-1), score.reshape(-1))


def solution(mesh):
    placed = (P("rows", "grp"), P(), P("rows"))
    return jax.shard_map(
        on_device,
        mesh=mesh,
        in_specs=placed,
        out_specs=(P(("rows", "grp")), P(("rows", "grp"))),
        check_vma=False,
    )
```

```python
import functools
import math

import jax
import jax.numpy as jnp
from jax import lax
from jax.experimental import pallas as pl
from jax.experimental.pallas import tpu as pltpu
from jax.sharding import PartitionSpec as P

MESH = pl.DeviceIdType.MESH
BLOCK = 256
SHARPNESS = 256.0
EPSILON = 1e-06
SCALE = SHARPNESS * math.log2(math.e)
MASKED = -1e30

NEXT1, NEXT2, NEXT3, PASS1, PASS2, VIA1, VIA2 = range(7)
Z_FIRST = (0, 3)
FIRST = 0
ORDER = (0, 1, 3, 2)


def as_row(column):
    return jnp.transpose(jnp.broadcast_to(column, (column.shape[0], 128)))[0:1, :]


def as_column(row):
    return jnp.transpose(jnp.broadcast_to(row, (128, row.shape[1])))[:, 0:1]


def merge(former, latter):
    top = jnp.maximum(former[0], latter[0])
    base = jnp.maximum(0.0, top)
    summed = former[1] * jnp.exp2(jnp.maximum(0.0, former[0]) - base) + latter[1] * jnp.exp2(
        jnp.maximum(0.0, latter[0]) - base
    )
    return (top, summed)


def kernel(
    runs,
    features,
    clusters,
    bands_in,
    top_out,
    score_out,
    whole,
    ahead,
    work,
    labels,
    key_msg,
    key_got,
    query_msg,
    query_got,
    bands,
    load_sem,
    label_sem,
    whole_send,
    whole_recv,
    pass_send,
    ahead_send,
    ahead_recv,
    key_send,
    key_recv,
    query_send,
    query_recv,
):
    p = lax.axis_index("rows")
    m = lax.axis_index("grp")
    core = m % 2
    column = p % 4
    ring = p - column

    def at(run, member):
        return {"rows": run, "grp": member}

    def mate(j):
        low = (m + j) % 2
        high = (m // 2 + j // 2) % 2
        return high * 2 + low

    def shifted(distance):
        return (p + distance + runs) % runs

    left = ring + (column + 3) % 4
    right = ring + (column + 1) % 4
    below = shifted(-4)
    above = shifted(4)
    layer = 32
    first_ring = (p // 4) % 8 == 0
    last_ring = (p // 4) % 8 == 7
    near, far = m // 2 == 0, m // 2 == 1

    loads = []
    for j in range(4):
        start = pl.multiple_of(mate(j) * BLOCK, BLOCK)
        loads.append(
            pltpu.make_async_copy(features.at[pl.ds(start, BLOCK)], whole.at[0, j], load_sem.at[j])
        )
    for j in (1, 3, 2, 0):
        loads[j].start()
    label_loads = []
    for i in range(4):
        start = pl.multiple_of(shifted(i) * 8, 8)
        label_loads.append(
            pltpu.make_async_copy(clusters.at[pl.ds(start, 8)], labels.at[i], label_sem.at[i])
        )
        label_loads[i].start()

    label_loads.append(pltpu.make_async_copy(bands_in, bands, label_sem.at[4]))
    label_loads[4].start()

    barrier = pltpu.get_barrier_semaphore()
    greeted = [at(p, mate(j)) for j in (1, 2, 3)]
    greeted += [at(run, m) for run in (left, right, above, shifted(-1), shifted(-2), shifted(-3))]
    for device in greeted:
        pl.semaphore_signal(barrier, inc=1, device_id=device, device_id_type=MESH)

    def greet(run, member):
        pl.semaphore_signal(barrier, inc=1, device_id=at(run, member), device_id_type=MESH)

    @pl.when(first_ring)
    def _():
        greet(shifted(layer), m)

        @pl.when(far)
        def _():
            greet(shifted(layer), mate(2))

    @pl.when(last_ring)
    def _():
        greet(shifted(4 - layer), m)

        @pl.when(far)
        def _():
            greet(above, mate(2))

    for j in range(4):
        loads[j].wait()
    extra = jnp.where(first_ring, jnp.where(near, 4, 2), 0)
    pl.semaphore_wait(barrier, len(greeted) + extra)

    def group_copy(piece, j, to_piece, to_j, partner, send_sem):
        return pltpu.make_async_remote_copy(
            src_ref=whole.at[piece, j],
            dst_ref=whole.at[to_piece, to_j],
            send_sem=send_sem,
            recv_sem=whole_recv.at[to_piece, to_j],
            device_id=at(p, mate(partner)),
            device_id_type=MESH,
        )

    def to_core(j):
        return group_copy(0, j, 1, j ^ 1, 1, whole_send.at[0, j])

    def to_chip(j):
        return group_copy(0, j, 2, j ^ 2, 2, whole_send.at[1, j])

    def pass_on(j):
        return group_copy(2, j, 3, j ^ 1, 1, pass_send.at[j])

    def arrived(piece, j):
        group_copy(0, j, piece, j, 1, whole_send.at[0, 0]).wait_recv()

    def ahead_copy(kind, source, r, run, slot, member=m):
        return pltpu.make_async_remote_copy(
            src_ref=source,
            dst_ref=ahead.at[slot, r],
            send_sem=ahead_send.at[kind, r],
            recv_sem=ahead_recv.at[slot, r],
            device_id=at(run, member),
            device_id_type=MESH,
        )

    def ahead_arrived(slot, r):
        ahead_copy(0, whole.at[0, 0], r, p, slot).wait_recv()

    even, odd = core == 0, core == 1
    drops = (even & (column < 3)) | (odd & (column < 2))

    def send_below(kind, source, r, slot, ring_kind):
        if ring_kind == FIRST and r in Z_FIRST:
            ahead_copy(kind, source, r, shifted(-layer), VIA1).start()
        else:
            ahead_copy(kind, source, r, below, slot).start()

    def send_own(r):
        own = whole.at[r, 0]

        @pl.when(column != 0)
        def _():
            ahead_copy(0, own, r, left, NEXT1).start()

        @pl.when((even & (column == 3)) | (odd & (column >= 2)))
        def _():
            slot = jnp.where(odd & (column == 2), PASS1, NEXT3)
            ahead_copy(2, own, r, right, slot).start()

        @pl.when(drops & ~first_ring)
        def _():
            send_below(3, own, r, PASS1, None)

        @pl.when(drops & first_ring & near)
        def _():
            send_below(3, own, r, PASS1, FIRST)

    def send_other(piece):
        r = piece ^ 2

        @pl.when(drops & first_ring & near)
        def _():
            if piece in (1, 3):
                arrived(piece, 2)
            run, slot = (shifted(-layer), VIA1) if r in Z_FIRST else (below, PASS1)
            ahead_copy(7, whole.at[piece, 2], r, run, slot, mate(2)).start()

    def relay_layer(r):
        @pl.when(drops)
        def _():
            ahead_arrived(VIA1, r)
            ahead_copy(5, ahead.at[VIA1, r], r, shifted(layer - 4), PASS1).start()

    def relay_layer_late(r):
        @pl.when(odd & (column == 3))
        def _():
            ahead_arrived(VIA1, r)
            ahead_copy(5, ahead.at[VIA1, r], r, shifted(layer - 4), NEXT3).start()

    def relay_pass(r):
        passing = ahead.at[PASS1, r]

        @pl.when(drops)
        def _():
            ahead_arrived(PASS1, r)
            ahead_copy(2, passing, r, right, NEXT3).start()

        @pl.when(column == 0)
        def _():
            ahead_copy(0, passing, r, left, NEXT1).start()

    def relay_cross(r, ring_kind):
        passing = ahead.at[PASS1, r]

        @pl.when(odd & (column == 3))
        def _():
            ahead_arrived(PASS1, r)
            send_below(3, passing, r, NEXT3, ring_kind)
            ahead_copy(1, passing, r, right, NEXT2).start()

    def relay_soon(r, ring_kind):
        @pl.when(even & (column < 3))
        def _():
            ahead_arrived(NEXT1, r)

            if ring_kind != FIRST:
                @pl.when(column == 0)
                def _():
                    ahead_copy(4, ahead.at[NEXT1, r], r, below, PASS2).start()

            @pl.when(column != 0)
            def _():
                ahead_copy(1, ahead.at[NEXT1, r], r, left, NEXT2).start()

        @pl.when(odd & (column == 0))
        def _():
            ahead_arrived(NEXT3, r)
            ahead_copy(1, ahead.at[NEXT3, r], r, right, NEXT2).start()

    def relay_later(r):
        @pl.when(even & (column == 3))
        def _():
            ahead_arrived(NEXT1, r)
            ahead_copy(1, ahead.at[NEXT1, r], r, left, NEXT2).start()

        @pl.when(odd & ((column == 1) | (column == 2)))
        def _():
            ahead_arrived(NEXT3, r)
            ahead_copy(1, ahead.at[NEXT3, r], r, right, NEXT2).start()

    def relay_last(r):
        @pl.when(even & (column == 2))
        def _():
            ahead_arrived(NEXT3, r)
            ahead_copy(4, ahead.at[NEXT3, r], r, right, NEXT2).start()

    def relay_second(r):
        @pl.when(even & (column == 0))
        def _():
            ahead_arrived(PASS2, r)
            ahead_copy(1, ahead.at[PASS2, r], r, left, NEXT2).start()

    def relay_rest(piece):
        arrived(2, piece)
        pass_on(piece).start()

    to_core(1).start()
    to_chip(3).start()
    to_chip(2).start()
    send_own(0)
    for j in (2, 0, 3):
        to_core(j).start()
    send_other(0)
    arrived(1, 0)
    send_own(1)
    send_other(1)

    @pl.when(~last_ring)
    def _():
        relay_pass(0)

    @pl.when(first_ring)
    def _():
        relay_layer(jnp.where(far, 3, 0))

    @pl.when(last_ring)
    def _():
        relay_soon(0, None)
        relay_cross(0, None)

    arrived(2, 1)
    pass_on(1).start()
    arrived(3, 0)
    send_own(3)

    @pl.when(~last_ring)
    def _():
        relay_pass(1)

    @pl.when(last_ring)
    def _():
        relay_pass(jnp.where(far, 2, 1))

    arrived(2, 0)
    send_own(2)
    pass_on(0).start()
    to_chip(3).wait_send()
    to_chip(2).wait_send()
    to_chip(1).start()
    to_chip(0).start()

    @pl.when(~first_ring & ~last_ring)
    def _():
        for r, then in ((3, 0), (2, 1)):
            relay_pass(r)
            relay_cross(then, None)
            relay_soon(then, None)
            relay_later(then)
        relay_rest(2)
        relay_cross(3, None)
        relay_soon(3, None)
        relay_later(3)
        relay_rest(3)
        relay_cross(2, None)
        relay_soon(2, None)
        relay_later(2)
        for r in ORDER:
            relay_second(r)

    @pl.when(first_ring)
    def _():
        relay_soon(0, FIRST)

        @pl.when(near)
        def _():
            relay_layer(3)

        relay_pass(3)
        relay_rest(2)
        send_other(2)
        relay_soon(1, FIRST)
        relay_rest(3)
        send_other(3)
        relay_pass(2)

        @pl.when(far)
        def _():
            relay_layer(0)

        relay_cross(0, FIRST)
        relay_cross(1, FIRST)
        for r in (3, 2):
            relay_soon(r, FIRST)
            relay_cross(r, FIRST)
        for r in ORDER:
            relay_later(r)
        relay_layer_late(0)
        relay_layer_late(3)
        for r in ORDER:
            relay_second(r)

    @pl.when(last_ring)
    def _():
        coming = [jnp.where(far, a, b) for a, b in zip((2, 3, 1, 0), (1, 0, 2, 3))]
        relay_soon(1, None)
        relay_cross(1, None)
        relay_pass(coming[1])
        relay_rest(2)
        relay_soon(3, None)
        relay_cross(3, None)
        relay_rest(3)
        relay_soon(2, None)
        relay_cross(2, None)
        relay_pass(coming[2])
        relay_later(coming[0])
        relay_pass(coming[3])
        for r in coming[1:]:
            relay_later(r)
        for r in coming:
            relay_last(r)

    for j in (1, 3):
        arrived(1, j)
        arrived(3, j)

    @pl.when(~(drops & first_ring & near))
    def _():
        arrived(1, 2)
        arrived(3, 2)

    for i in range(5):
        label_loads[i].wait()

    def inverse_norm(blocks):
        squares = [jnp.square(b.astype(jnp.float32)) for b in blocks]
        return lax.rsqrt(
            jnp.sum(squares[0] + squares[1] + squares[2] + squares[3], axis=1, keepdims=True)
            + EPSILON
        )

    def label_row(i, block):
        return jnp.concatenate(
            [labels[i, pl.ds(2 * block, 1), :], labels[i, pl.ds(2 * block + 1, 1), :]], axis=1
        )

    query_inv, query_label = [], []
    own_inv = None
    for j in range(4):
        inv = inverse_norm([whole[r, j] for r in range(4)])
        own_inv = inv if j == 0 else own_inv
        query_inv.append(as_row(inv))
        query_label.append(label_row(0, mate(j)))

    def tile(i, keys, inv):
        label = as_column(label_row(i, m).astype(jnp.float32)).astype(jnp.int32)
        label = jnp.where(p + i < runs, label, -2)
        key_scale = inv * SCALE
        key_top = jnp.full((BLOCK, 1), MASKED, jnp.float32)
        key_sum = jnp.zeros((BLOCK, 1), jnp.float32)
        tops = []
        for j in range(4):
            products = None
            for r in range(4):
                term = lax.dot_general(
                    keys[r], whole[r, j], (((1,), (1,)), ((), ())), preferred_element_type=jnp.float32
                )
                products = term if products is None else products + term
            block = mate(j)
            if i > 0:
                valid = 4 * i + m - block <= bands[block]
            elif j > 0:
                valid = jnp.where(block > m, block - m <= bands[m], m - block <= bands[block])
            else:
                valid = True
            query = query_label[j] if valid is True else jnp.where(valid, query_label[j], -1)
            chosen = label == query
            if i == 0 and j == 0:
                rows = lax.broadcasted_iota(jnp.int32, (BLOCK, BLOCK), 0)
                columns = lax.broadcasted_iota(jnp.int32, (BLOCK, BLOCK), 1)
                chosen = chosen & (rows != columns)
            scaled = jnp.where(chosen, products * key_scale * query_inv[j], MASKED)
            work[:, j * BLOCK : (j + 1) * BLOCK] = scaled
            key_top = jnp.maximum(key_top, jnp.max(scaled, axis=1, keepdims=True))
            if i > 0:
                tops.append(jnp.max(scaled, axis=0, keepdims=True))
        key_base = jnp.maximum(0.0, key_top)
        sums = []
        for j in range(4):
            scaled = work[:, j * BLOCK : (j + 1) * BLOCK]
            key_sum += jnp.sum(jnp.exp2(scaled - key_base), axis=1, keepdims=True)
            if i > 0:
                base = jnp.maximum(0.0, tops[j])
                sums.append(jnp.sum(jnp.exp2(scaled - base), axis=0, keepdims=True))
        return (as_row(key_top), as_row(key_sum)), list(zip(tops, sums))

    own, _ = tile(0, [whole[r, 0] for r in range(4)], own_inv)

    def key_copy(i):
        return pltpu.make_async_remote_copy(
            src_ref=key_msg.at[i - 1],
            dst_ref=key_got.at[i - 1],
            send_sem=key_send.at[i - 1],
            recv_sem=key_recv.at[i - 1],
            device_id=at(shifted(i), m),
            device_id_type=MESH,
        )

    def query_copy(j):
        return pltpu.make_async_remote_copy(
            src_ref=query_msg.at[j - 1],
            dst_ref=query_got.at[j - 1],
            send_sem=query_send.at[j - 1],
            recv_sem=query_recv.at[j - 1],
            device_id=at(p, mate(j)),
            device_id_type=MESH,
        )

    running = None
    for i, slot in ((1, NEXT1), (3, NEXT3), (2, NEXT2)):
        for r in ORDER:
            if slot == NEXT1:
                @pl.when(odd)
                def _():
                    ahead_arrived(NEXT1, r)
            elif slot == NEXT3:
                @pl.when((even & ~((column == 2) & last_ring)) | (odd & (column == 3)))
                def _():
                    ahead_arrived(NEXT3, r)
            else:
                ahead_arrived(NEXT2, r)
        keys = [ahead[slot, r] for r in range(4)]
        key_stats, query_stats = tile(i, keys, inverse_norm(keys))
        key_msg[i - 1, 0:1, :] = key_stats[0]
        key_msg[i - 1, 1:2, :] = key_stats[1]
        key_copy(i).start()
        if running is None:
            running = query_stats
        else:
            running = [merge(a, b) for a, b in zip(running, query_stats)]

    for j in (3, 2, 1):
        query_msg[j - 1, 0:1, :] = running[j][0]
        query_msg[j - 1, 1:2, :] = running[j][1]
        query_copy(j).start()
    state = merge(own, running[0])

    def sent(kind, r):
        ahead_copy(kind, whole.at[0, 0], r, p, NEXT1).wait_send()

    for r in range(4):
        sent(0, r)
        sent(2, r)

        @pl.when(~(last_ring & even & (column == 0)))
        def _():
            sent(1, r)

        @pl.when((drops & ~(first_ring & far)) | (odd & (column == 3)))
        def _():
            sent(3, r)

        @pl.when(drops & first_ring & near)
        def _():
            sent(7, r)

        @pl.when(even & (((column == 0) & ~first_ring) | ((column == 2) & last_ring)))
        def _():
            sent(4, r)

        if r in Z_FIRST:
            @pl.when(first_ring & (drops | (odd & (column == 3))))
            def _():
                sent(5, r)

    for j in range(4):
        to_core(j).wait_send()
        pass_on(j).wait_send()
    to_chip(1).wait_send()
    to_chip(0).wait_send()
    for i in (1, 3, 2):
        key_copy(i).wait()
        state = merge(state, (key_got[i - 1, 0:1, :], key_got[i - 1, 1:2, :]))
    for j in (1, 2, 3):
        query_copy(j).wait()
        state = merge(state, (query_got[j - 1, 0:1, :], query_got[j - 1, 1:2, :]))
    top, summed = state
    base = jnp.maximum(0.0, top)
    top_out[...] = jnp.maximum(-1.0, top * (1.0 / SCALE))
    score_out[...] = base * math.log(2.0) + jnp.log(jnp.exp2(-base) + summed)


def on_device(features, clusters, bands):
    runs = lax.axis_size("rows")
    rows, width = features.shape
    dma = pltpu.SemaphoreType.DMA
    top, score = pl.pallas_call(
        functools.partial(kernel, runs),
        out_shape=[jax.ShapeDtypeStruct((1, BLOCK), jnp.float32)] * 2,
        in_specs=[
            pl.BlockSpec(memory_space=pltpu.HBM),
            pl.BlockSpec(memory_space=pltpu.HBM),
            pl.BlockSpec(memory_space=pltpu.HBM),
        ],
        out_specs=[pl.BlockSpec(memory_space=pltpu.VMEM)] * 2,
        scratch_shapes=[
            pltpu.VMEM((4, 4, BLOCK, width), jnp.bfloat16),
            pltpu.VMEM((7, 4, BLOCK, width), jnp.bfloat16),
            pltpu.VMEM((BLOCK, rows), jnp.float32),
            pltpu.VMEM((4, 8, 128), jnp.int32),
            pltpu.VMEM((3, 8, BLOCK), jnp.float32),
            pltpu.VMEM((3, 8, BLOCK), jnp.float32),
            pltpu.VMEM((3, 8, BLOCK), jnp.float32),
            pltpu.VMEM((3, 8, BLOCK), jnp.float32),
            pltpu.SMEM((4,), jnp.int32),
            dma((4,)),
            dma((5,)),
            dma((2, 4)),
            dma((4, 4)),
            dma((4,)),
            dma((8, 4)),
            dma((7, 4)),
            dma((3,)),
            dma((3,)),
            dma((3,)),
            dma((3,)),
        ],
        compiler_params=pltpu.CompilerParams(
            collective_id=0, has_side_effects=True, vmem_limit_bytes=60 * 1024 * 1024
        ),
        name="screen",
    )(features, clusters.reshape(-1, 128), bands)
    return (top.reshape(-1), score.reshape(-1))


def solution(mesh):
    placed = (P("rows", "grp"), P(), P("rows"))
    return jax.shard_map(
        on_device,
        mesh=mesh,
        in_specs=placed,
        out_specs=(P(("rows", "grp")), P(("rows", "grp"))),
        check_vma=False,
    )
```

```python
import functools
import math

import jax
import jax.numpy as jnp
from jax import lax
from jax.experimental import pallas as pl
from jax.experimental.pallas import tpu as pltpu
from jax.sharding import PartitionSpec as P

MESH = pl.DeviceIdType.MESH
BLOCK = 256
SHARPNESS = 256.0
EPSILON = 1e-06
SCALE = SHARPNESS * math.log2(math.e)
MASKED = -1e30

NEXT1, NEXT2, NEXT3, PASS1, PASS2, VIA1, VIA2 = range(7)
Z_FIRST = (0, 3)
FIRST = 0
ORDER = (0, 1, 3, 2)


def as_row(column):
    return jnp.transpose(jnp.broadcast_to(column, (column.shape[0], 128)))[0:1, :]


def as_column(row):
    return jnp.transpose(jnp.broadcast_to(row, (128, row.shape[1])))[:, 0:1]


def merge(former, latter):
    top = jnp.maximum(former[0], latter[0])
    base = jnp.maximum(0.0, top)
    summed = former[1] * jnp.exp2(jnp.maximum(0.0, former[0]) - base) + latter[1] * jnp.exp2(
        jnp.maximum(0.0, latter[0]) - base
    )
    return (top, summed)


def kernel(
    runs,
    features,
    clusters,
    bands_in,
    top_out,
    score_out,
    whole,
    ahead,
    work,
    labels,
    key_msg,
    key_got,
    query_msg,
    query_got,
    bands,
    load_sem,
    label_sem,
    whole_send,
    whole_recv,
    pass_send,
    ahead_send,
    ahead_recv,
    key_send,
    key_recv,
    query_send,
    query_recv,
):
    p = lax.axis_index("rows")
    m = lax.axis_index("grp")
    core = m % 2
    column = p % 4
    ring = p - column

    def at(run, member):
        return {"rows": run, "grp": member}

    def mate(j):
        low = (m + j) % 2
        high = (m // 2 + j // 2) % 2
        return high * 2 + low

    def shifted(distance):
        return (p + distance + runs) % runs

    left = ring + (column + 3) % 4
    right = ring + (column + 1) % 4
    below = shifted(-4)
    above = shifted(4)
    layer = 32
    first_ring = (p // 4) % 8 == 0
    last_ring = (p // 4) % 8 == 7
    near, far = m // 2 == 0, m // 2 == 1

    loads = []
    for j in range(4):
        start = pl.multiple_of(mate(j) * BLOCK, BLOCK)
        loads.append(
            pltpu.make_async_copy(features.at[pl.ds(start, BLOCK)], whole.at[0, j], load_sem.at[j])
        )
    for j in (1, 3, 2, 0):
        loads[j].start()
    label_loads = []
    for i in range(4):
        start = pl.multiple_of(shifted(i) * 8, 8)
        label_loads.append(
            pltpu.make_async_copy(clusters.at[pl.ds(start, 8)], labels.at[i], label_sem.at[i])
        )
        label_loads[i].start()

    label_loads.append(pltpu.make_async_copy(bands_in, bands, label_sem.at[4]))
    label_loads[4].start()

    barrier = pltpu.get_barrier_semaphore()
    greeted = [at(p, mate(j)) for j in (1, 2, 3)]
    greeted += [at(run, m) for run in (left, right, above, shifted(-1), shifted(-2), shifted(-3))]
    for device in greeted:
        pl.semaphore_signal(barrier, inc=1, device_id=device, device_id_type=MESH)

    def greet(run, member):
        pl.semaphore_signal(barrier, inc=1, device_id=at(run, member), device_id_type=MESH)

    @pl.when(first_ring)
    def _():
        greet(shifted(layer), m)

        @pl.when(far)
        def _():
            greet(shifted(layer), mate(2))

    @pl.when(last_ring)
    def _():
        greet(shifted(4 - layer), m)

        @pl.when(far)
        def _():
            greet(above, mate(2))

    for j in range(4):
        loads[j].wait()
    extra = jnp.where(first_ring, jnp.where(near, 4, 2), 0)
    pl.semaphore_wait(barrier, len(greeted) + extra)

    def group_copy(piece, j, to_piece, to_j, partner, send_sem):
        return pltpu.make_async_remote_copy(
            src_ref=whole.at[piece, j],
            dst_ref=whole.at[to_piece, to_j],
            send_sem=send_sem,
            recv_sem=whole_recv.at[to_piece, to_j],
            device_id=at(p, mate(partner)),
            device_id_type=MESH,
        )

    def to_core(j):
        return group_copy(0, j, 1, j ^ 1, 1, whole_send.at[0, j])

    def to_chip(j):
        return group_copy(0, j, 2, j ^ 2, 2, whole_send.at[1, j])

    def pass_on(j):
        return group_copy(2, j, 3, j ^ 1, 1, pass_send.at[j])

    def arrived(piece, j):
        group_copy(0, j, piece, j, 1, whole_send.at[0, 0]).wait_recv()

    def ahead_copy(kind, source, r, run, slot, member=m):
        return pltpu.make_async_remote_copy(
            src_ref=source,
            dst_ref=ahead.at[slot, r],
            send_sem=ahead_send.at[kind, r],
            recv_sem=ahead_recv.at[slot, r],
            device_id=at(run, member),
            device_id_type=MESH,
        )

    def ahead_arrived(slot, r):
        ahead_copy(0, whole.at[0, 0], r, p, slot).wait_recv()

    even, odd = core == 0, core == 1
    drops = (even & (column < 3)) | (odd & (column < 2))

    def send_below(kind, source, r, slot, ring_kind):
        if ring_kind == FIRST and r in Z_FIRST:
            ahead_copy(kind, source, r, shifted(-layer), VIA1).start()
        else:
            ahead_copy(kind, source, r, below, slot).start()

    def send_own(r):
        own = whole.at[r, 0]

        @pl.when(column != 0)
        def _():
            ahead_copy(0, own, r, left, NEXT1).start()

        @pl.when((even & (column == 3)) | (odd & (column >= 2)))
        def _():
            slot = jnp.where(odd & (column == 2), PASS1, NEXT3)
            ahead_copy(2, own, r, right, slot).start()

        @pl.when(drops & ~first_ring)
        def _():
            send_below(3, own, r, PASS1, None)

        @pl.when(drops & first_ring & (near if r > 1 else True))
        def _():
            send_below(3, own, r, PASS1, FIRST)

    def send_other(piece):
        r = piece ^ 2

        @pl.when(drops & first_ring & near)
        def _():
            if piece == 1:
                arrived(piece, 2)
            run, slot = (shifted(-layer), VIA1) if r in Z_FIRST else (below, PASS1)
            ahead_copy(7, whole.at[piece, 2], r, run, slot, mate(2)).start()

    def relay_layer(r):
        @pl.when(drops)
        def _():
            ahead_arrived(VIA1, r)
            ahead_copy(5, ahead.at[VIA1, r], r, shifted(layer - 4), PASS1).start()

    def relay_layer_late(r):
        @pl.when(odd & (column == 3))
        def _():
            ahead_arrived(VIA1, r)
            ahead_copy(5, ahead.at[VIA1, r], r, shifted(layer - 4), NEXT3).start()

    def relay_pass(r):
        passing = ahead.at[PASS1, r]

        @pl.when(drops)
        def _():
            ahead_arrived(PASS1, r)
            ahead_copy(2, passing, r, right, NEXT3).start()

        @pl.when(column == 0)
        def _():
            ahead_copy(0, passing, r, left, NEXT1).start()

    def relay_cross(r, ring_kind):
        passing = ahead.at[PASS1, r]

        @pl.when(odd & (column == 3))
        def _():
            ahead_arrived(PASS1, r)
            send_below(3, passing, r, NEXT3, ring_kind)
            ahead_copy(1, passing, r, right, NEXT2).start()

    def relay_soon(r, ring_kind):
        @pl.when(even & (column < 3))
        def _():
            ahead_arrived(NEXT1, r)

            if ring_kind != FIRST:
                @pl.when(column == 0)
                def _():
                    ahead_copy(4, ahead.at[NEXT1, r], r, below, PASS2).start()

            @pl.when(column != 0)
            def _():
                ahead_copy(1, ahead.at[NEXT1, r], r, left, NEXT2).start()

        @pl.when(odd & (column == 0))
        def _():
            ahead_arrived(NEXT3, r)
            ahead_copy(1, ahead.at[NEXT3, r], r, right, NEXT2).start()

    def relay_later(r):
        @pl.when(even & (column == 3))
        def _():
            ahead_arrived(NEXT1, r)
            ahead_copy(1, ahead.at[NEXT1, r], r, left, NEXT2).start()

        @pl.when(odd & ((column == 1) | (column == 2)))
        def _():
            ahead_arrived(NEXT3, r)
            ahead_copy(1, ahead.at[NEXT3, r], r, right, NEXT2).start()

    def relay_last(r):
        @pl.when(even & (column == 2))
        def _():
            ahead_arrived(NEXT3, r)
            ahead_copy(4, ahead.at[NEXT3, r], r, right, NEXT2).start()

    def relay_second(r):
        @pl.when(even & (column == 0))
        def _():
            ahead_arrived(PASS2, r)
            ahead_copy(1, ahead.at[PASS2, r], r, left, NEXT2).start()

    def relay_rest(piece):
        arrived(2, piece)
        pass_on(piece).start()

    to_core(1).start()
    to_chip(3).start()
    to_chip(2).start()
    send_own(0)
    for j in (2, 0, 3):
        to_core(j).start()
    send_other(0)
    arrived(1, 0)
    send_own(1)
    send_other(1)

    @pl.when(~last_ring)
    def _():
        relay_pass(0)

    @pl.when(first_ring)
    def _():
        relay_layer(jnp.where(far, 3, 0))

    @pl.when(last_ring)
    def _():
        relay_soon(0, None)
        relay_cross(0, None)

    arrived(2, 1)
    pass_on(1).start()
    arrived(3, 0)
    send_own(3)

    @pl.when(~last_ring)
    def _():
        relay_pass(1)

    @pl.when(last_ring)
    def _():
        relay_pass(jnp.where(far, 2, 1))

    arrived(2, 0)
    send_own(2)
    pass_on(0).start()
    to_chip(3).wait_send()
    to_chip(2).wait_send()
    to_chip(1).start()
    to_chip(0).start()

    @pl.when(~first_ring & ~last_ring)
    def _():
        for r, then in ((3, 0), (2, 1)):
            relay_pass(r)
            relay_cross(then, None)
            relay_soon(then, None)
            relay_later(then)
        relay_rest(2)
        relay_cross(3, None)
        relay_soon(3, None)
        relay_later(3)
        relay_rest(3)
        relay_cross(2, None)
        relay_soon(2, None)
        relay_later(2)
        for r in ORDER:
            relay_second(r)

    @pl.when(first_ring)
    def _():
        relay_soon(0, FIRST)

        @pl.when(near)
        def _():
            relay_layer(3)

        relay_pass(3)
        relay_soon(1, FIRST)

        @pl.when(far)
        def _():
            relay_layer(0)

        relay_pass(2)
        relay_cross(0, FIRST)
        relay_cross(1, FIRST)
        for r in (3, 2):
            relay_soon(r, FIRST)
            relay_cross(r, FIRST)
        for r in ORDER:
            relay_later(r)
        relay_layer_late(0)
        relay_rest(2)
        relay_rest(3)
        relay_layer_late(3)
        for r in ORDER:
            relay_second(r)

    @pl.when(last_ring)
    def _():
        coming = [jnp.where(far, a, b) for a, b in zip((2, 3, 1, 0), (1, 0, 2, 3))]
        relay_soon(1, None)
        relay_cross(1, None)
        relay_pass(coming[1])
        relay_soon(3, None)
        relay_cross(3, None)
        relay_pass(coming[2])
        relay_later(coming[0])
        relay_soon(2, None)
        relay_cross(2, None)
        relay_pass(coming[3])
        relay_later(coming[1])
        relay_last(coming[0])
        relay_later(coming[2])
        relay_last(coming[1])
        relay_later(coming[3])
        relay_rest(2)
        relay_rest(3)
        relay_last(coming[2])
        relay_last(coming[3])

    for j in (1, 2, 3):
        arrived(3, j)
    for j in (1, 3):
        arrived(1, j)

    @pl.when(~(drops & first_ring & near))
    def _():
        arrived(1, 2)

    for i in range(5):
        label_loads[i].wait()

    def inverse_norm(blocks):
        squares = [jnp.square(b.astype(jnp.float32)) for b in blocks]
        return lax.rsqrt(
            jnp.sum(squares[0] + squares[1] + squares[2] + squares[3], axis=1, keepdims=True)
            + EPSILON
        )

    def label_row(i, block):
        return jnp.concatenate(
            [labels[i, pl.ds(2 * block, 1), :], labels[i, pl.ds(2 * block + 1, 1), :]], axis=1
        )

    query_inv, query_label = [], []
    own_inv = None
    for j in range(4):
        inv = inverse_norm([whole[r, j] for r in range(4)])
        own_inv = inv if j == 0 else own_inv
        query_inv.append(as_row(inv))
        query_label.append(label_row(0, mate(j)))

    def tile(i, keys, inv):
        label = as_column(label_row(i, m).astype(jnp.float32)).astype(jnp.int32)
        label = jnp.where(p + i < runs, label, -2)
        key_scale = inv * SCALE
        key_top = jnp.full((BLOCK, 1), MASKED, jnp.float32)
        key_sum = jnp.zeros((BLOCK, 1), jnp.float32)
        tops = []
        for j in range(4):
            products = None
            for r in range(4):
                term = lax.dot_general(
                    keys[r], whole[r, j], (((1,), (1,)), ((), ())), preferred_element_type=jnp.float32
                )
                products = term if products is None else products + term
            block = mate(j)
            if i > 0:
                valid = 4 * i + m - block <= bands[block]
            elif j > 0:
                valid = jnp.where(block > m, block - m <= bands[m], m - block <= bands[block])
            else:
                valid = True
            query = query_label[j] if valid is True else jnp.where(valid, query_label[j], -1)
            chosen = label == query
            if i == 0 and j == 0:
                rows = lax.broadcasted_iota(jnp.int32, (BLOCK, BLOCK), 0)
                columns = lax.broadcasted_iota(jnp.int32, (BLOCK, BLOCK), 1)
                chosen = chosen & (rows != columns)
            scaled = jnp.where(chosen, products * key_scale * query_inv[j], MASKED)
            work[:, j * BLOCK : (j + 1) * BLOCK] = scaled
            key_top = jnp.maximum(key_top, jnp.max(scaled, axis=1, keepdims=True))
            if i > 0:
                tops.append(jnp.max(scaled, axis=0, keepdims=True))
        key_base = jnp.maximum(0.0, key_top)
        sums = []
        for j in range(4):
            scaled = work[:, j * BLOCK : (j + 1) * BLOCK]
            key_sum += jnp.sum(jnp.exp2(scaled - key_base), axis=1, keepdims=True)
            if i > 0:
                base = jnp.maximum(0.0, tops[j])
                sums.append(jnp.sum(jnp.exp2(scaled - base), axis=0, keepdims=True))
        return (as_row(key_top), as_row(key_sum)), list(zip(tops, sums))

    own, _ = tile(0, [whole[r, 0] for r in range(4)], own_inv)

    def key_copy(i):
        return pltpu.make_async_remote_copy(
            src_ref=key_msg.at[i - 1],
            dst_ref=key_got.at[i - 1],
            send_sem=key_send.at[i - 1],
            recv_sem=key_recv.at[i - 1],
            device_id=at(shifted(i), m),
            device_id_type=MESH,
        )

    def query_copy(j):
        return pltpu.make_async_remote_copy(
            src_ref=query_msg.at[j - 1],
            dst_ref=query_got.at[j - 1],
            send_sem=query_send.at[j - 1],
            recv_sem=query_recv.at[j - 1],
            device_id=at(p, mate(j)),
            device_id_type=MESH,
        )

    running = None
    for i, slot in ((1, NEXT1), (3, NEXT3), (2, NEXT2)):
        for r in ORDER:
            if slot == NEXT1:
                @pl.when(odd)
                def _():
                    ahead_arrived(NEXT1, r)
            elif slot == NEXT3:
                @pl.when((even & ~((column == 2) & last_ring)) | (odd & (column == 3)))
                def _():
                    ahead_arrived(NEXT3, r)
            else:
                ahead_arrived(NEXT2, r)
        keys = [ahead[slot, r] for r in range(4)]
        key_stats, query_stats = tile(i, keys, inverse_norm(keys))
        key_msg[i - 1, 0:1, :] = key_stats[0]
        key_msg[i - 1, 1:2, :] = key_stats[1]

        @pl.when(p + i < runs)
        def _():
            key_copy(i).start()

        if running is None:
            running = query_stats
        else:
            running = [merge(a, b) for a, b in zip(running, query_stats)]

    for j in (3, 2, 1):
        query_msg[j - 1, 0:1, :] = running[j][0]
        query_msg[j - 1, 1:2, :] = running[j][1]
        query_copy(j).start()
    state = merge(own, running[0])

    def sent(kind, r):
        ahead_copy(kind, whole.at[0, 0], r, p, NEXT1).wait_send()

    for r in range(4):
        sent(0, r)
        sent(2, r)

        @pl.when(~(last_ring & even & (column == 0)))
        def _():
            sent(1, r)

        @pl.when((drops & (~(first_ring & far) if r > 1 else True)) | (odd & (column == 3)))
        def _():
            sent(3, r)

        if r > 1:
            @pl.when(drops & first_ring & near)
            def _():
                sent(7, r)

        @pl.when(even & (((column == 0) & ~first_ring) | ((column == 2) & last_ring)))
        def _():
            sent(4, r)

        if r in Z_FIRST:
            @pl.when(first_ring & (drops | (odd & (column == 3))))
            def _():
                sent(5, r)

    for j in range(4):
        to_core(j).wait_send()
        pass_on(j).wait_send()
    to_chip(1).wait_send()
    to_chip(0).wait_send()
    for i in (1, 3, 2):
        @pl.when(p + i < runs)
        def _():
            key_copy(i).wait_send()

        @pl.when(p >= i)
        def _():
            key_copy(i).wait_recv()

        @pl.when(p < i)
        def _():
            key_got[i - 1, 0:1, :] = jnp.full((1, BLOCK), MASKED, jnp.float32)
            key_got[i - 1, 1:2, :] = jnp.zeros((1, BLOCK), jnp.float32)

        state = merge(state, (key_got[i - 1, 0:1, :], key_got[i - 1, 1:2, :]))
    for j in (1, 2, 3):
        query_copy(j).wait()
        state = merge(state, (query_got[j - 1, 0:1, :], query_got[j - 1, 1:2, :]))
    top, summed = state
    base = jnp.maximum(0.0, top)
    top_out[...] = jnp.maximum(-1.0, top * (1.0 / SCALE))
    score_out[...] = base * math.log(2.0) + jnp.log(jnp.exp2(-base) + summed)


def on_device(features, clusters, bands):
    runs = lax.axis_size("rows")
    rows, width = features.shape
    dma = pltpu.SemaphoreType.DMA
    top, score = pl.pallas_call(
        functools.partial(kernel, runs),
        out_shape=[jax.ShapeDtypeStruct((1, BLOCK), jnp.float32)] * 2,
        in_specs=[
            pl.BlockSpec(memory_space=pltpu.HBM),
            pl.BlockSpec(memory_space=pltpu.HBM),
            pl.BlockSpec(memory_space=pltpu.HBM),
        ],
        out_specs=[pl.BlockSpec(memory_space=pltpu.VMEM)] * 2,
        scratch_shapes=[
            pltpu.VMEM((4, 4, BLOCK, width), jnp.bfloat16),
            pltpu.VMEM((7, 4, BLOCK, width), jnp.bfloat16),
            pltpu.VMEM((BLOCK, rows), jnp.float32),
            pltpu.VMEM((4, 8, 128), jnp.int32),
            pltpu.VMEM((3, 8, BLOCK), jnp.float32),
            pltpu.VMEM((3, 8, BLOCK), jnp.float32),
            pltpu.VMEM((3, 8, BLOCK), jnp.float32),
            pltpu.VMEM((3, 8, BLOCK), jnp.float32),
            pltpu.SMEM((4,), jnp.int32),
            dma((4,)),
            dma((5,)),
            dma((2, 4)),
            dma((4, 4)),
            dma((4,)),
            dma((8, 4)),
            dma((7, 4)),
            dma((3,)),
            dma((3,)),
            dma((3,)),
            dma((3,)),
        ],
        compiler_params=pltpu.CompilerParams(
            collective_id=0, has_side_effects=True, vmem_limit_bytes=60 * 1024 * 1024
        ),
        name="screen",
    )(features, clusters.reshape(-1, 128), bands)
    return (top.reshape(-1), score.reshape(-1))


def solution(mesh):
    placed = (P("rows", "grp"), P(), P("rows"))
    return jax.shard_map(
        on_device,
        mesh=mesh,
        in_specs=placed,
        out_specs=(P(("rows", "grp")), P(("rows", "grp"))),
        check_vma=False,
    )
```

```python
import functools
import math

import jax
import jax.numpy as jnp
from jax import lax
from jax.experimental import pallas as pl
from jax.experimental.pallas import tpu as pltpu
from jax.sharding import PartitionSpec as P

MESH = pl.DeviceIdType.MESH
BLOCK = 256
SHARPNESS = 256.0
EPSILON = 1e-06
SCALE = SHARPNESS * math.log2(math.e)
MASKED = -1e30

NEXT1, NEXT2, NEXT3, PASS1, PASS2, VIA1, VIA2 = range(7)
Z_FIRST = (0, 3)
FIRST = 0
ORDER = (0, 1, 3, 2)


def as_row(column):
    return jnp.transpose(jnp.broadcast_to(column, (column.shape[0], 128)))[0:1, :]


def as_column(row):
    return jnp.transpose(jnp.broadcast_to(row, (128, row.shape[1])))[:, 0:1]


def merge(former, latter):
    top = jnp.maximum(former[0], latter[0])
    base = jnp.maximum(0.0, top)
    summed = former[1] * jnp.exp2(jnp.maximum(0.0, former[0]) - base) + latter[1] * jnp.exp2(
        jnp.maximum(0.0, latter[0]) - base
    )
    return (top, summed)


def kernel(
    runs,
    features,
    clusters,
    bands_in,
    top_out,
    score_out,
    whole,
    ahead,
    work,
    labels,
    key_msg,
    key_got,
    query_msg,
    query_got,
    bands,
    load_sem,
    label_sem,
    whole_send,
    whole_recv,
    pass_send,
    ahead_send,
    ahead_recv,
    key_send,
    key_recv,
    query_send,
    query_recv,
):
    p = lax.axis_index("rows")
    m = lax.axis_index("grp")
    core = m % 2
    column = p % 4
    ring = p - column

    def at(run, member):
        return {"rows": run, "grp": member}

    def mate(j):
        low = (m + j) % 2
        high = (m // 2 + j // 2) % 2
        return high * 2 + low

    def shifted(distance):
        return (p + distance + runs) % runs

    left = ring + (column + 3) % 4
    right = ring + (column + 1) % 4
    below = shifted(-4)
    above = shifted(4)
    layer = 32
    first_ring = (p // 4) % 8 == 0
    last_ring = (p // 4) % 8 == 7
    near, far = m // 2 == 0, m // 2 == 1

    loads = []
    for j in range(4):
        start = pl.multiple_of(mate(j) * BLOCK, BLOCK)
        loads.append(
            pltpu.make_async_copy(features.at[pl.ds(start, BLOCK)], whole.at[0, j], load_sem.at[j])
        )
    for j in (1, 3, 2, 0):
        loads[j].start()
    label_loads = []
    for i in range(4):
        start = pl.multiple_of(shifted(i) * 8, 8)
        label_loads.append(
            pltpu.make_async_copy(clusters.at[pl.ds(start, 8)], labels.at[i], label_sem.at[i])
        )
        label_loads[i].start()

    label_loads.append(pltpu.make_async_copy(bands_in, bands, label_sem.at[4]))
    label_loads[4].start()

    barrier = pltpu.get_barrier_semaphore()
    greeted = [at(p, mate(j)) for j in (1, 2, 3)]
    greeted += [at(run, m) for run in (left, right, above, shifted(-1), shifted(-2), shifted(-3))]
    for device in greeted:
        pl.semaphore_signal(barrier, inc=1, device_id=device, device_id_type=MESH)

    def greet(run, member):
        pl.semaphore_signal(barrier, inc=1, device_id=at(run, member), device_id_type=MESH)

    @pl.when(first_ring)
    def _():
        greet(shifted(layer), m)

        @pl.when(far)
        def _():
            greet(shifted(layer), mate(2))

    @pl.when(last_ring)
    def _():
        greet(shifted(4 - layer), m)

        @pl.when(far)
        def _():
            greet(above, mate(2))

    for j in range(4):
        loads[j].wait()
    extra = jnp.where(first_ring, jnp.where(near, 4, 2), 0)
    pl.semaphore_wait(barrier, len(greeted) + extra)

    def group_copy(piece, j, to_piece, to_j, partner, send_sem):
        return pltpu.make_async_remote_copy(
            src_ref=whole.at[piece, j],
            dst_ref=whole.at[to_piece, to_j],
            send_sem=send_sem,
            recv_sem=whole_recv.at[to_piece, to_j],
            device_id=at(p, mate(partner)),
            device_id_type=MESH,
        )

    def to_core(j):
        return group_copy(0, j, 1, j ^ 1, 1, whole_send.at[0, j])

    def to_chip(j):
        return group_copy(0, j, 2, j ^ 2, 2, whole_send.at[1, j])

    def pass_on(j):
        return group_copy(2, j, 3, j ^ 1, 1, pass_send.at[j])

    def arrived(piece, j):
        group_copy(0, j, piece, j, 1, whole_send.at[0, 0]).wait_recv()

    def ahead_copy(kind, source, r, run, slot, member=m):
        return pltpu.make_async_remote_copy(
            src_ref=source,
            dst_ref=ahead.at[slot, r],
            send_sem=ahead_send.at[kind, r],
            recv_sem=ahead_recv.at[slot, r],
            device_id=at(run, member),
            device_id_type=MESH,
        )

    def ahead_arrived(slot, r):
        ahead_copy(0, whole.at[0, 0], r, p, slot).wait_recv()

    even, odd = core == 0, core == 1
    drops = (even & (column < 3)) | (odd & (column < 2))

    def send_below(kind, source, r, slot, ring_kind):
        if ring_kind == FIRST and r in Z_FIRST:
            ahead_copy(kind, source, r, shifted(-layer), VIA1).start()
        else:
            ahead_copy(kind, source, r, below, slot).start()

    def send_own(r):
        own = whole.at[r, 0]

        @pl.when(column != 0)
        def _():
            ahead_copy(0, own, r, left, NEXT1).start()

        @pl.when((even & (column == 3)) | (odd & (column >= 2)))
        def _():
            slot = jnp.where(odd & (column == 2), PASS1, NEXT3)
            ahead_copy(2, own, r, right, slot).start()

        @pl.when(drops & ~first_ring)
        def _():
            send_below(3, own, r, PASS1, None)

        @pl.when(drops & first_ring & (near if r > 1 else True))
        def _():
            send_below(3, own, r, PASS1, FIRST)

    def send_other(piece):
        r = piece ^ 2

        @pl.when(drops & first_ring & near)
        def _():
            if piece == 1:
                arrived(piece, 2)
            run, slot = (shifted(-layer), VIA1) if r in Z_FIRST else (below, PASS1)
            ahead_copy(7, whole.at[piece, 2], r, run, slot, mate(2)).start()

    def relay_layer(r):
        @pl.when(drops)
        def _():
            ahead_arrived(VIA1, r)
            ahead_copy(5, ahead.at[VIA1, r], r, shifted(layer - 4), PASS1).start()

    def relay_layer_late(r):
        @pl.when(odd & (column == 3))
        def _():
            ahead_arrived(VIA1, r)
            ahead_copy(5, ahead.at[VIA1, r], r, shifted(layer - 4), NEXT3).start()

    def relay_pass(r):
        passing = ahead.at[PASS1, r]

        @pl.when(drops)
        def _():
            ahead_arrived(PASS1, r)
            ahead_copy(2, passing, r, right, NEXT3).start()

        @pl.when(column == 0)
        def _():
            ahead_copy(0, passing, r, left, NEXT1).start()

    def relay_cross(r, ring_kind):
        passing = ahead.at[PASS1, r]

        @pl.when(odd & (column == 3))
        def _():
            ahead_arrived(PASS1, r)
            send_below(3, passing, r, NEXT3, ring_kind)
            ahead_copy(1, passing, r, right, NEXT2).start()

    def relay_soon(r, ring_kind):
        @pl.when(even & (column < 3))
        def _():
            ahead_arrived(NEXT1, r)

            if ring_kind != FIRST:
                @pl.when(column == 0)
                def _():
                    ahead_copy(4, ahead.at[NEXT1, r], r, below, PASS2).start()

            @pl.when(column != 0)
            def _():
                ahead_copy(1, ahead.at[NEXT1, r], r, left, NEXT2).start()

        @pl.when(odd & (column == 0))
        def _():
            ahead_arrived(NEXT3, r)
            ahead_copy(1, ahead.at[NEXT3, r], r, right, NEXT2).start()

    def relay_later(r):
        @pl.when(even & (column == 3))
        def _():
            ahead_arrived(NEXT1, r)
            ahead_copy(1, ahead.at[NEXT1, r], r, left, NEXT2).start()

        @pl.when(odd & ((column == 1) | (column == 2)))
        def _():
            ahead_arrived(NEXT3, r)
            ahead_copy(1, ahead.at[NEXT3, r], r, right, NEXT2).start()

    def relay_last(r):
        @pl.when(even & (column == 2))
        def _():
            ahead_arrived(NEXT3, r)
            ahead_copy(4, ahead.at[NEXT3, r], r, right, NEXT2).start()

    def relay_second(r):
        @pl.when(even & (column == 0))
        def _():
            ahead_arrived(PASS2, r)
            ahead_copy(1, ahead.at[PASS2, r], r, left, NEXT2).start()

    def relay_rest(piece):
        arrived(2, piece)
        pass_on(piece).start()

    def inverse_norm(blocks):
        squares = [jnp.square(b.astype(jnp.float32)) for b in blocks]
        return lax.rsqrt(
            jnp.sum(squares[0] + squares[1] + squares[2] + squares[3], axis=1, keepdims=True)
            + EPSILON
        )

    to_core(1).start()
    to_chip(3).start()
    to_chip(2).start()
    send_own(0)
    for j in (2, 0, 3):
        to_core(j).start()
    send_other(0)
    arrived(1, 0)
    send_own(1)
    send_other(1)

    @pl.when(~last_ring)
    def _():
        relay_pass(0)

    @pl.when(first_ring)
    def _():
        relay_layer(jnp.where(far, 3, 0))

    @pl.when(last_ring)
    def _():
        relay_soon(0, None)
        relay_cross(0, None)

    arrived(2, 1)
    pass_on(1).start()
    arrived(3, 0)
    send_own(3)

    @pl.when(~last_ring)
    def _():
        relay_pass(1)

    @pl.when(last_ring)
    def _():
        relay_pass(jnp.where(far, 2, 1))

    arrived(2, 0)
    send_own(2)
    pass_on(0).start()
    to_chip(3).wait_send()
    to_chip(2).wait_send()
    to_chip(1).start()
    to_chip(0).start()
    early_norms = []
    arrived(1, 1)
    arrived(3, 1)
    for j in range(2):
        early_norms.append(inverse_norm([whole[r, j] for r in range(4)]))

    @pl.when(~first_ring & ~last_ring)
    def _():
        for r, then in ((3, 0), (2, 1)):
            relay_pass(r)
            relay_cross(then, None)
            relay_soon(then, None)
            relay_later(then)
        relay_rest(2)
        relay_cross(3, None)
        relay_soon(3, None)
        relay_later(3)
        relay_rest(3)
        relay_cross(2, None)
        relay_soon(2, None)
        relay_later(2)
        for r in ORDER:
            relay_second(r)

    @pl.when(first_ring)
    def _():
        relay_soon(0, FIRST)

        @pl.when(near)
        def _():
            relay_layer(3)

        relay_pass(3)
        relay_soon(1, FIRST)

        @pl.when(far)
        def _():
            relay_layer(0)

        relay_pass(2)
        relay_cross(0, FIRST)
        relay_cross(1, FIRST)
        for r in (3, 2):
            relay_soon(r, FIRST)
            relay_cross(r, FIRST)
        for r in ORDER:
            relay_later(r)
        relay_layer_late(0)
        relay_rest(2)
        relay_rest(3)
        relay_layer_late(3)
        for r in ORDER:
            relay_second(r)

    @pl.when(last_ring)
    def _():
        coming = [jnp.where(far, a, b) for a, b in zip((2, 3, 1, 0), (1, 0, 2, 3))]
        relay_soon(1, None)
        relay_cross(1, None)
        relay_pass(coming[1])
        relay_soon(3, None)
        relay_cross(3, None)
        relay_pass(coming[2])
        relay_later(coming[0])
        relay_soon(2, None)
        relay_cross(2, None)
        relay_pass(coming[3])
        relay_later(coming[1])
        relay_last(coming[0])
        relay_later(coming[2])
        relay_last(coming[1])
        relay_later(coming[3])
        relay_rest(2)
        relay_rest(3)
        relay_last(coming[2])
        relay_last(coming[3])

    for j in (2, 3):
        arrived(3, j)
    arrived(1, 3)

    @pl.when(~(drops & first_ring & near))
    def _():
        arrived(1, 2)

    for i in range(5):
        label_loads[i].wait()

    def label_row(i, block):
        return jnp.concatenate(
            [labels[i, pl.ds(2 * block, 1), :], labels[i, pl.ds(2 * block + 1, 1), :]], axis=1
        )

    query_inv, query_label = [], []
    own_inv = None
    for j in range(4):
        inv = early_norms[j] if j < 2 else inverse_norm([whole[r, j] for r in range(4)])
        own_inv = inv if j == 0 else own_inv
        query_inv.append(as_row(inv))
        query_label.append(label_row(0, mate(j)))

    def tile(i, keys, inv):
        label = as_column(label_row(i, m).astype(jnp.float32)).astype(jnp.int32)
        label = jnp.where(p + i < runs, label, -2)
        key_scale = inv * SCALE
        key_top = jnp.full((BLOCK, 1), MASKED, jnp.float32)
        key_sum = jnp.zeros((BLOCK, 1), jnp.float32)
        tops = []
        for j in range(4):
            products = None
            for r in range(4):
                term = lax.dot_general(
                    keys[r], whole[r, j], (((1,), (1,)), ((), ())), preferred_element_type=jnp.float32
                )
                products = term if products is None else products + term
            block = mate(j)
            if i > 0:
                valid = 4 * i + m - block <= bands[block]
            elif j > 0:
                valid = jnp.where(block > m, block - m <= bands[m], m - block <= bands[block])
            else:
                valid = True
            query = query_label[j] if valid is True else jnp.where(valid, query_label[j], -1)
            chosen = label == query
            if i == 0 and j == 0:
                rows = lax.broadcasted_iota(jnp.int32, (BLOCK, BLOCK), 0)
                columns = lax.broadcasted_iota(jnp.int32, (BLOCK, BLOCK), 1)
                chosen = chosen & (rows != columns)
            scaled = jnp.where(chosen, products * key_scale * query_inv[j], MASKED)
            work[:, j * BLOCK : (j + 1) * BLOCK] = scaled
            key_top = jnp.maximum(key_top, jnp.max(scaled, axis=1, keepdims=True))
            if i > 0:
                tops.append(jnp.max(scaled, axis=0, keepdims=True))
        key_base = jnp.maximum(0.0, key_top)
        sums = []
        for j in range(4):
            scaled = work[:, j * BLOCK : (j + 1) * BLOCK]
            key_sum += jnp.sum(jnp.exp2(scaled - key_base), axis=1, keepdims=True)
            if i > 0:
                base = jnp.maximum(0.0, tops[j])
                sums.append(jnp.sum(jnp.exp2(scaled - base), axis=0, keepdims=True))
        return (as_row(key_top), as_row(key_sum)), list(zip(tops, sums))

    own, _ = tile(0, [whole[r, 0] for r in range(4)], own_inv)

    def key_copy(i):
        return pltpu.make_async_remote_copy(
            src_ref=key_msg.at[i - 1],
            dst_ref=key_got.at[i - 1],
            send_sem=key_send.at[i - 1],
            recv_sem=key_recv.at[i - 1],
            device_id=at(shifted(i), m),
            device_id_type=MESH,
        )

    def query_copy(j):
        return pltpu.make_async_remote_copy(
            src_ref=query_msg.at[j - 1],
            dst_ref=query_got.at[j - 1],
            send_sem=query_send.at[j - 1],
            recv_sem=query_recv.at[j - 1],
            device_id=at(p, mate(j)),
            device_id_type=MESH,
        )

    running = None
    for i, slot in ((1, NEXT1), (3, NEXT3), (2, NEXT2)):
        for r in ORDER:
            if slot == NEXT1:
                @pl.when(odd)
                def _():
                    ahead_arrived(NEXT1, r)
            elif slot == NEXT3:
                @pl.when((even & ~((column == 2) & last_ring)) | (odd & (column == 3)))
                def _():
                    ahead_arrived(NEXT3, r)
            else:
                ahead_arrived(NEXT2, r)
        keys = [ahead[slot, r] for r in range(4)]
        key_stats, query_stats = tile(i, keys, inverse_norm(keys))
        key_msg[i - 1, 0:1, :] = key_stats[0]
        key_msg[i - 1, 1:2, :] = key_stats[1]

        @pl.when(p + i < runs)
        def _():
            key_copy(i).start()

        if running is None:
            running = query_stats
        else:
            running = [merge(a, b) for a, b in zip(running, query_stats)]

    for j in (3, 2, 1):
        query_msg[j - 1, 0:1, :] = running[j][0]
        query_msg[j - 1, 1:2, :] = running[j][1]
        query_copy(j).start()
    state = merge(own, running[0])

    def sent(kind, r):
        ahead_copy(kind, whole.at[0, 0], r, p, NEXT1).wait_send()

    for r in range(4):
        sent(0, r)
        sent(2, r)

        @pl.when(~(last_ring & even & (column == 0)))
        def _():
            sent(1, r)

        @pl.when((drops & (~(first_ring & far) if r > 1 else True)) | (odd & (column == 3)))
        def _():
            sent(3, r)

        if r > 1:
            @pl.when(drops & first_ring & near)
            def _():
                sent(7, r)

        @pl.when(even & (((column == 0) & ~first_ring) | ((column == 2) & last_ring)))
        def _():
            sent(4, r)

        if r in Z_FIRST:
            @pl.when(first_ring & (drops | (odd & (column == 3))))
            def _():
                sent(5, r)

    for j in range(4):
        to_core(j).wait_send()
        pass_on(j).wait_send()
    to_chip(1).wait_send()
    to_chip(0).wait_send()
    for i in (1, 3, 2):
        @pl.when(p + i < runs)
        def _():
            key_copy(i).wait_send()

        @pl.when(p >= i)
        def _():
            key_copy(i).wait_recv()

        @pl.when(p < i)
        def _():
            key_got[i - 1, 0:1, :] = jnp.full((1, BLOCK), MASKED, jnp.float32)
            key_got[i - 1, 1:2, :] = jnp.zeros((1, BLOCK), jnp.float32)

        state = merge(state, (key_got[i - 1, 0:1, :], key_got[i - 1, 1:2, :]))
    for j in (1, 2, 3):
        query_copy(j).wait()
        state = merge(state, (query_got[j - 1, 0:1, :], query_got[j - 1, 1:2, :]))
    top, summed = state
    base = jnp.maximum(0.0, top)
    top_out[...] = jnp.maximum(-1.0, top * (1.0 / SCALE))
    score_out[...] = base * math.log(2.0) + jnp.log(jnp.exp2(-base) + summed)


def on_device(features, clusters, bands):
    runs = lax.axis_size("rows")
    rows, width = features.shape
    dma = pltpu.SemaphoreType.DMA
    top, score = pl.pallas_call(
        functools.partial(kernel, runs),
        out_shape=[jax.ShapeDtypeStruct((1, BLOCK), jnp.float32)] * 2,
        in_specs=[
            pl.BlockSpec(memory_space=pltpu.HBM),
            pl.BlockSpec(memory_space=pltpu.HBM),
            pl.BlockSpec(memory_space=pltpu.HBM),
        ],
        out_specs=[pl.BlockSpec(memory_space=pltpu.VMEM)] * 2,
        scratch_shapes=[
            pltpu.VMEM((4, 4, BLOCK, width), jnp.bfloat16),
            pltpu.VMEM((7, 4, BLOCK, width), jnp.bfloat16),
            pltpu.VMEM((BLOCK, rows), jnp.float32),
            pltpu.VMEM((4, 8, 128), jnp.int32),
            pltpu.VMEM((3, 8, BLOCK), jnp.float32),
            pltpu.VMEM((3, 8, BLOCK), jnp.float32),
            pltpu.VMEM((3, 8, BLOCK), jnp.float32),
            pltpu.VMEM((3, 8, BLOCK), jnp.float32),
            pltpu.SMEM((4,), jnp.int32),
            dma((4,)),
            dma((5,)),
            dma((2, 4)),
            dma((4, 4)),
            dma((4,)),
            dma((8, 4)),
            dma((7, 4)),
            dma((3,)),
            dma((3,)),
            dma((3,)),
            dma((3,)),
        ],
        compiler_params=pltpu.CompilerParams(
            collective_id=0, has_side_effects=True, vmem_limit_bytes=60 * 1024 * 1024
        ),
        name="screen",
    )(features, clusters.reshape(-1, 128), bands)
    return (top.reshape(-1), score.reshape(-1))


def solution(mesh):
    placed = (P("rows", "grp"), P(), P("rows"))
    return jax.shard_map(
        on_device,
        mesh=mesh,
        in_specs=placed,
        out_specs=(P(("rows", "grp")), P(("rows", "grp"))),
        check_vma=False,
    )
```
